32 devices in a mesh: seq: 8 (over z, x), fsdp: 4 (over y, core).
Axes of the slice: x: 2, y: 2, z: 4, core: 2. Of those that a mesh axis runs over, the one named last changes fastest.
Arguments:
- tokens: bfloat16 [4, 1024, 4608], P('fsdp', 'seq'), may hold values from -6 to 6
- norm_gain: float32 [4608], replicated, may hold values from 0.3 to 3
- router_weight: float32 [4608], replicated, may hold values from -0.09375 to 0.09375
- w_query: bfloat16 [4608, 1024], P('fsdp', 'seq'), may hold values from -0.09375 to 0.09375
- w_key: bfloat16 [4608, 1024], P('fsdp', 'seq'), may hold values from -0.09375 to 0.09375
- w_value: bfloat16 [4608, 1024], P('fsdp', 'seq'), may hold values from -0.09375 to 0.09375
- w_out: bfloat16 [1024, 4608], P('seq', 'fsdp'), may hold values from -0.1875 to 0.1875
- cotangent: bfloat16 [4, 1024, 4608], P('fsdp', 'seq'), may hold values from -6 to 6
- kept_index: int32 [4, 8, 24], P('fsdp', 'seq'), may hold values from -1 to 127, as said below
Outputs:
- mixed_rows: bfloat16 [4, 1024, 4608], P('fsdp', 'seq')
- grad_tokens: bfloat16 [4, 1024, 4608], P('fsdp', 'seq')
- grad_query: float32 [4608, 1024], P('fsdp', 'seq')
- grad_key: float32 [4608, 1024], P('fsdp', 'seq')
- grad_value: float32 [4608, 1024], P('fsdp', 'seq')
- grad_out: float32 [1024, 4608], P('seq', 'fsdp')
- grad_gain: float32 [4608], replicated
- grad_router: float32 [4608], replicated
The draws below stay inside these ranges and needn't reach their ends.
Inputs may be any that keep to these rules, and one draw needn't show every extreme that they name: `kept_index`: each row of a document and index of seq lists distinct increasing local positions, followed by -1 in its empty slots. Every document keeps exactly 128 tokens in all, and in every document some index of seq fills all 24 slots.
All inputs are finite; a program needn't handle non-finite values.
Results may differ from the reference program's by a relative error of at most 0.012.
The reference program's roundings to bfloat16 on the way count: a program that leaves them out, or rounds other values in their place, can miss the bound.
Values may be sent and summed in bfloat16 or wider, within the bound.
A program may use at most 64 MiB of HBM per device.

```python
import math
import jax
import jax.numpy as jnp
from jax import lax

D = 4608
HEAD_SIZE = 128
TOK_DEV = 128
HEADS = 8
HD = 1024
CAP = 24
SEQ_LEN = 1024
DOCS = 4
N_SEQ = 8


def draw_kept_index(key, part):
    key = jax.random.fold_in(key, 7)
    half_count = N_SEQ // 2
    mean_keep = TOK_DEV // 8
    spread = CAP - mean_keep

    def one_shard(shard_key, count):
        order = jax.random.permutation(shard_key, TOK_DEV)[:CAP]
        slot_number = jnp.arange(CAP, dtype=jnp.int32)
        chosen = jnp.where(slot_number < count, order, TOK_DEV)
        chosen = jnp.sort(chosen)
        return jnp.where(chosen < TOK_DEV, chosen, -1).astype(jnp.int32)

    def one_document(doc_key):
        first_key, second_key, third_key = jax.random.split(doc_key, 3)
        order = jax.random.permutation(first_key, N_SEQ)
        delta = jax.random.randint(second_key, (half_count,), 0, spread + 1)
        delta = delta.at[0].set(spread)
        counts = jnp.zeros((N_SEQ,), jnp.int32)
        counts = counts.at[order[:half_count]].set(mean_keep + delta)
        counts = counts.at[order[half_count:]].set(mean_keep - delta)
        shard_keys = jax.random.split(third_key, N_SEQ)
        return jax.vmap(one_shard)(shard_keys, counts)
    return jax.vmap(one_document)(jax.random.split(key, DOCS))


def steps_of(rng, dims, shards, low, top_value):
    loudness = 1.0
    for axis_at, blocks in shards:
        steps = jax.random.uniform(jax.random.fold_in(jax.random.fold_in(rng, 6), axis_at), (blocks,), jnp.float32, low / len(shards), top_value / len(shards))
        loudness = loudness * jnp.repeat(jnp.exp(steps), dims[axis_at] // blocks).reshape((-1,) + (1,) * (len(dims) - 1 - axis_at))
    return loudness


def bell_draw(own_key, dims, scale, limit, cuts=(), held_as=jnp.bfloat16):
    factor_of = steps_of(own_key, dims, cuts, -0.22, 0.18) if cuts else 1.0
    array = jax.random.normal(own_key, dims, jnp.float32) * scale * factor_of
    return jnp.minimum(jnp.maximum(array, -limit), limit).astype(held_as)


def setup_inputs(seed: int = 0) -> dict:
    key_list = jax.random.split(jax.random.key(seed), 10)
    return {
        "tokens": bell_draw(key_list[0], (DOCS, SEQ_LEN, D), 1.0, 6.0, ((0, 4), (1, 8))),
        "norm_gain": jnp.clip(jnp.exp(jax.random.uniform(key_list[1], (D,), jnp.float32, math.log(0.3), math.log(3.0))), 0.3, 3.0),
        "router_weight": bell_draw(key_list[2], (D,), D ** -0.5, 0.09375, (), jnp.float32),
        "w_query": bell_draw(key_list[3], (D, HD), D ** -0.5, 0.09375, ((0, 4), (1, 8))),
        "w_key": bell_draw(key_list[4], (D, HD), D ** -0.5, 0.09375, ((0, 4), (1, 8))),
        "w_value": bell_draw(key_list[5], (D, HD), D ** -0.5, 0.09375, ((0, 4), (1, 8))),
        "w_out": bell_draw(key_list[6], (HD, D), HD ** -0.5, 0.1875, ((0, 8), (1, 4))),
        "cotangent": bell_draw(key_list[7], (DOCS, SEQ_LEN, D), 1.0, 6.0, ((0, 4), (1, 8))),
        "kept_index": draw_kept_index(jax.random.fold_in(key_list[9], 71), 0),
    }


SOFTCAP = 50.0
QUERY_SCALE = 1.0 / 12.0
FAR = 2 ** 30
EPS = 1e-06

def rounded(values):
    return lax.optimization_barrier(values.astype(jnp.bfloat16)).astype(jnp.float32)

def reference(tokens, norm_gain, router_weight, w_query, w_key, w_value, w_out, cotangent, kept_index):
    slot_total = N_SEQ * CAP
    width = HEADS * HEAD_SIZE
    out_heads = w_out.astype(jnp.float32).reshape(HEADS, HEAD_SIZE, D)
    query_heads_w = w_query.astype(jnp.float32).reshape(D, HEADS, HEAD_SIZE)
    key_heads_w = w_key.astype(jnp.float32).reshape(D, HEADS, HEAD_SIZE)
    value_heads_w = w_value.astype(jnp.float32).reshape(D, HEADS, HEAD_SIZE)

    def one_document(totals, inputs):
        doc_tokens, doc_cotangent, doc_slots = inputs
        is_kept = doc_slots >= 0
        offsets = (jnp.arange(N_SEQ, dtype=jnp.int32) * TOK_DEV)[:, None]
        rows = jnp.where(is_kept, doc_slots + offsets, 0).reshape(-1).astype(jnp.int32)
        kept_flat = is_kept.reshape(-1)
        position = jnp.where(kept_flat, rows, FAR).astype(jnp.int32)
        target = jnp.where(kept_flat, rows, N_SEQ * TOK_DEV).astype(jnp.int32)
        kept_rows = jnp.where(kept_flat[:, None], doc_tokens[rows], jnp.zeros((), jnp.bfloat16))
        kept_float = kept_rows.astype(jnp.float32)
        inv_root = lax.rsqrt(lax.optimization_barrier(jnp.mean(kept_float * kept_float, axis=1)) + EPS)
        unit = kept_float * inv_root[:, None]
        normed = (unit * norm_gain).astype(jnp.bfloat16)
        queries = jnp.dot(normed, w_query, preferred_element_type=jnp.float32).astype(jnp.bfloat16)
        keys_all = jnp.dot(normed, w_key, preferred_element_type=jnp.float32).astype(jnp.bfloat16)
        values_all = jnp.dot(normed, w_value, preferred_element_type=jnp.float32).astype(jnp.bfloat16)
        query_heads = queries.astype(jnp.float32).reshape(slot_total, HEADS, HEAD_SIZE)
        key_heads = keys_all.astype(jnp.float32).reshape(slot_total, HEADS, HEAD_SIZE)
        value_heads = values_all.astype(jnp.float32).reshape(slot_total, HEADS, HEAD_SIZE)
        raw_scores = jnp.einsum('qhs,khs->hqk', query_heads, key_heads) * QUERY_SCALE
        capped = SOFTCAP * jnp.tanh(raw_scores / SOFTCAP)
        allowed = (position[None, :] <= position[:, None]) & (position[None, :] < FAR)
        powers = jnp.where(allowed[None], jnp.exp(capped), 0.0)
        softmax_values = powers / lax.optimization_barrier(jnp.sum(powers, axis=2, keepdims=True))
        rounded_weights = softmax_values.astype(jnp.bfloat16)
        weights_float = rounded_weights.astype(jnp.float32)
        attended = jnp.einsum('hqk,khs->qhs', weights_float, value_heads).astype(jnp.bfloat16)
        attended_float = attended.astype(jnp.float32)
        head_terms = rounded(jnp.einsum('qhs,hsd->hqd', attended_float, out_heads))
        mixed_sum = lax.optimization_barrier(jnp.sum(head_terms, axis=0))
        logits = jnp.dot(kept_float, router_weight, precision=lax.Precision.HIGHEST)
        gate_value = jax.nn.sigmoid(logits)
        new_rows = (kept_float + gate_value[:, None] * mixed_sum).astype(jnp.bfloat16)
        doc_mixed = doc_tokens.at[target].set(new_rows, mode='drop')
        cot_rows = jnp.where(kept_flat[:, None], doc_cotangent[rows], jnp.zeros((), jnp.bfloat16)).astype(jnp.float32)
        d_gate = lax.optimization_barrier(jnp.sum(cot_rows * mixed_sum, axis=1))
        d_logit = d_gate * gate_value * (1.0 - gate_value)
        d_mix = (gate_value[:, None] * cot_rows).astype(jnp.bfloat16)
        out_term = jnp.dot(attended.reshape(slot_total, width).T, d_mix, preferred_element_type=jnp.float32)
        d_attended = jnp.einsum('qd,hsd->qhs', d_mix.astype(jnp.float32), out_heads).astype(jnp.bfloat16)
        d_att_float = d_attended.astype(jnp.float32)
        d_values = jnp.einsum('hqk,qhs->khs', weights_float, d_att_float).astype(jnp.bfloat16)
        d_probs = jnp.einsum('qhs,khs->hqk', d_att_float, value_heads)
        d_soft = softmax_values * (d_probs - lax.optimization_barrier(jnp.sum(softmax_values * d_probs, axis=2, keepdims=True)))
        d_raw = (d_soft * (1.0 - capped / SOFTCAP * (capped / SOFTCAP)) * QUERY_SCALE).astype(jnp.bfloat16)
        d_raw_float = d_raw.astype(jnp.float32)
        d_queries = jnp.einsum('hqk,khs->qhs', d_raw_float, key_heads).astype(jnp.bfloat16)
        d_keys = jnp.einsum('hqk,qhs->khs', d_raw_float, query_heads).astype(jnp.bfloat16)
        query_term = jnp.dot(normed.T, d_queries.reshape(slot_total, width), preferred_element_type=jnp.float32)
        key_term = jnp.dot(normed.T, d_keys.reshape(slot_total, width), preferred_element_type=jnp.float32)
        value_term = jnp.dot(normed.T, d_values.reshape(slot_total, width), preferred_element_type=jnp.float32)
        input_terms = jnp.einsum('qhs,dhs->hqd', d_queries.astype(jnp.float32), query_heads_w)
        input_terms = input_terms + jnp.einsum('qhs,dhs->hqd', d_keys.astype(jnp.float32), key_heads_w)
        input_terms = input_terms + jnp.einsum('qhs,dhs->hqd', d_values.astype(jnp.float32), value_heads_w)
        d_normed = lax.optimization_barrier(jnp.sum(rounded(input_terms), axis=0))
        gain_term = lax.optimization_barrier(jnp.sum(d_normed * unit, axis=0))
        router_term = lax.optimization_barrier(jnp.sum(d_logit[:, None] * kept_float, axis=0))
        scaled = d_normed * norm_gain
        d_kept = inv_root[:, None] * (scaled - unit * lax.optimization_barrier(jnp.mean(scaled * unit, axis=1, keepdims=True)))
        grad_new = (cot_rows + d_kept + d_logit[:, None] * router_weight).astype(jnp.bfloat16)
        doc_grad = doc_cotangent.at[target].set(grad_new, mode='drop')
        totals = (totals[0] + query_term, totals[1] + key_term, totals[2] + value_term, totals[3] + out_term, totals[4] + gain_term, totals[5] + router_term)
        return (totals, (doc_mixed, doc_grad))
    start = (jnp.zeros((D, width), jnp.float32), jnp.zeros((D, width), jnp.float32), jnp.zeros((D, width), jnp.float32), jnp.zeros((width, D), jnp.float32), jnp.zeros((D,), jnp.float32), jnp.zeros((D,), jnp.float32))
    totals, outputs = lax.scan(one_document, start, (tokens, cotangent, kept_index))
    return (outputs[0], outputs[1], totals[0], totals[1], totals[2], totals[3], totals[4], totals[5])
```

```python
import functools

import jax
import jax.numpy as jnp
from jax import lax
from jax.experimental import pallas as pl
from jax.experimental.pallas import tpu as pltpu
from jax.sharding import PartitionSpec as P

SOFTCAP = 50.0
QUERY_SCALE = 1.0 / 12.0
EPS = 1e-06
MESH = pl.DeviceIdType.MESH
VMEM_LIMIT = 48 * 1024 * 1024


def contract_rows(left, right):
    return lax.dot_general(
        left, right, (((0,), (0,)), ((), ())), preferred_element_type=jnp.float32
    )


def contract_cols(left, right):
    return lax.dot_general(
        left, right, (((1,), (1,)), ((), ())), preferred_element_type=jnp.float32
    )


def place(axis, size):
    me = lax.axis_index(axis)
    return me, me // 2, lax.rem(me, 2), size // 2


def pair_peers(axis, size):
    me, outer, inner, outers = place(axis, size)
    peers = [{axis: lax.rem(outer + d, outers) * 2 + inner} for d in range(1, outers)]
    peers.append({axis: outer * 2 + 1 - inner})
    return peers


def all_peers(axis, size):
    me = lax.axis_index(axis)
    return [{axis: lax.rem(me + d, size)} for d in range(1, size)]


def meet(peers):
    barrier = pltpu.get_barrier_semaphore()
    for peer in peers:
        pl.semaphore_signal(barrier, inc=1, device_id=peer, device_id_type=MESH)
    pl.semaphore_wait(barrier, len(peers))


def remote(src, dst, send, recv, peer):
    return pltpu.make_async_remote_copy(
        src_ref=src, dst_ref=dst, send_sem=send, recv_sem=recv, device_id=peer, device_id_type=MESH
    )


def gather_start(axis, size, src, dst, sems, own_sem):
    me, outer, inner, outers = place(axis, size)
    own = pltpu.make_async_copy(src, dst.at[me], own_sem)
    first = []
    for d in range(1, outers):
        peer = {axis: lax.rem(outer + d, outers) * 2 + inner}
        first.append(remote(src, dst.at[me], sems.at[0, d], sems.at[1, d], peer))
    partner = {axis: outer * 2 + 1 - inner}
    second = [remote(src, dst.at[me], sems.at[2, 0], sems.at[3, 0], partner)]
    for copy in first + second:
        copy.start()
    own.start()
    return own, first, second


def gather_forward(axis, size, dst, sems, copies):
    me, outer, inner, outers = place(axis, size)
    own, first, second = copies
    partner = {axis: outer * 2 + 1 - inner}
    for d in range(1, outers):
        first[d - 1].wait_recv()
        block = lax.rem(outer + outers - d, outers) * 2 + inner
        copy = remote(dst.at[block], dst.at[block], sems.at[2, d], sems.at[3, d], partner)
        copy.start()
        second.append(copy)


def gather_finish(copies):
    own, first, second = copies
    own.wait()
    for copy in first:
        copy.wait_send()
    for copy in second:
        copy.wait()


def gather_kernel(plan, *refs):
    count = len(plan)
    srcs, dsts = refs[:count], refs[count : 2 * count]
    sems, own_sems = refs[2 * count : 3 * count], refs[3 * count]
    peers = []
    for axis, size in dict(plan).items():
        peers += pair_peers(axis, size)
    meet(peers)
    running = [
        gather_start(axis, size, src, dst, sem, own_sems.at[i])
        for i, ((axis, size), src, dst, sem) in enumerate(zip(plan, srcs, dsts, sems))
    ]
    for (axis, size), dst, sem, copies in zip(plan, dsts, sems, running):
        gather_forward(axis, size, dst, sem, copies)
    for copies in running:
        gather_finish(copies)


def gather(plan, arrays, collective_id):
    return pl.pallas_call(
        functools.partial(gather_kernel, plan),
        out_shape=[
            jax.ShapeDtypeStruct((size,) + a.shape, a.dtype) for (_, size), a in zip(plan, arrays)
        ],
        in_specs=[pl.BlockSpec(memory_space=pl.ANY)] * len(arrays),
        out_specs=[pl.BlockSpec(memory_space=pl.ANY)] * len(arrays),
        scratch_shapes=[pltpu.SemaphoreType.DMA((4, size // 2)) for _, size in plan]
        + [pltpu.SemaphoreType.DMA((len(arrays),))],
        compiler_params=pltpu.CompilerParams(
            collective_id=collective_id, has_side_effects=True, vmem_limit_bytes=VMEM_LIMIT
        ),
        name="gather",
    )(*arrays)


def row_chunks(rows, run):
    if rows <= 32:
        run(slice(None))
        return
    step = next(s for s in (96, 64, 48, 32, 16) if rows % s == 0)

    @pl.loop(0, rows // step)
    def _(i):
        run(pl.ds(pl.multiple_of(i * step, step), step))


def scatter_start(axis, size, part, first_in, sems):
    me, outer, inner, outers = place(axis, size)
    partner = {axis: outer * 2 + 1 - inner}
    first = []
    for d in list(range(1, outers)) + [0]:
        to = lax.rem(outer + d, outers)
        copy = remote(
            part.at[to * 2 + 1 - inner], first_in.at[d], sems.at[0, d], sems.at[1, d], partner
        )
        copy.start()
        first.append((d, copy))
    return first


def scatter_step(axis, size, part, first_in, pair, second_in, sems, d, copy):
    me, outer, inner, outers = place(axis, size)
    to = lax.rem(outer + d, outers)
    copy.wait_recv()
    if d == 0:
        return None

    def run(rows):
        total = part[to * 2 + inner, rows].astype(jnp.float32) + first_in[d, rows].astype(
            jnp.float32
        )
        pair[d, rows] = total.astype(pair.dtype)

    row_chunks(part.shape[1], run)
    out = remote(
        pair.at[d], second_in.at[d], sems.at[2, d], sems.at[3, d], {axis: to * 2 + inner}
    )
    out.start()
    return out


def scatter_finish(axis, size, part, first_in, second_in, first, second, store):
    me, outer, inner, outers = place(axis, size)
    for copy in second:
        copy.wait()

    def run(rows):
        total = part[me, rows].astype(jnp.float32) + first_in[0, rows].astype(jnp.float32)
        for d in range(1, outers):
            total = total + second_in[d, rows].astype(jnp.float32)
        store(rows, total)

    row_chunks(part.shape[1], run)
    for _, copy in first:
        copy.wait_send()


def reduce_kernel(plan, splits, *refs):
    count, outs = len(plan), sum(splits)
    parts, out_refs, scratch = refs[:count], refs[count : count + outs], refs[count + outs :]
    peers = []
    for axis, size in dict(plan).items():
        peers += pair_peers(axis, size)
    meet(peers)
    held = [scratch[4 * i : 4 * i + 4] for i in range(count)]
    firsts = [
        scatter_start(axis, size, part, bufs[0], bufs[3])
        for (axis, size), part, bufs in zip(plan, parts, held)
    ]
    seconds = [[] for _ in plan]
    for turn in range(max(len(f) for f in firsts)):
        for i, (axis, size) in enumerate(plan):
            if turn < len(firsts[i]):
                d, copy = firsts[i][turn]
                first_in, pair, second_in, sems = held[i]
                out = scatter_step(
                    axis, size, parts[i], first_in, pair, second_in, sems, d, copy
                )
                if out is not None:
                    seconds[i].append(out)
    at = 0
    for i, (axis, size) in enumerate(plan):
        mine = out_refs[at : at + splits[i]]
        at += splits[i]

        def store(rows, total, mine=mine):
            width = total.shape[1] // len(mine)
            for j, ref in enumerate(mine):
                ref[rows] = total[:, j * width : (j + 1) * width]

        scatter_finish(
            axis, size, parts[i], held[i][0], held[i][2], firsts[i], seconds[i], store
        )


def reduce(plan, splits, arrays, collective_id):
    outs, scratch = [], []
    for (_, size), split, a in zip(plan, splits, arrays):
        outs += [jax.ShapeDtypeStruct((a.shape[1], a.shape[2] // split), jnp.float32)] * split
        scratch += [pltpu.VMEM((size // 2,) + a.shape[1:], a.dtype)] * 3
        scratch += [pltpu.SemaphoreType.DMA((4, size // 2))]
    return pl.pallas_call(
        functools.partial(reduce_kernel, plan, splits),
        out_shape=outs,
        in_specs=[pl.BlockSpec(memory_space=pltpu.VMEM)] * len(arrays),
        out_specs=[pl.BlockSpec(memory_space=pltpu.VMEM)] * len(outs),
        scratch_shapes=scratch,
        compiler_params=pltpu.CompilerParams(
            collective_id=collective_id, has_side_effects=True, vmem_limit_bytes=VMEM_LIMIT
        ),
        name="reduce",
    )(*arrays)


def exchange(axis, size, src, slots, sems):
    me = lax.axis_index(axis)
    copies = []
    for d in range(1, size):
        copies.append(
            remote(
                src, slots.at[me], sems.at[0, d], sems.at[1, d], {axis: lax.rem(me + d, size)}
            )
        )
    for copy in copies:
        copy.start()
    slots[me] = src[...]
    for copy in copies:
        copy.wait()
    total = slots[0]
    for s in range(1, size):
        total = total + slots[s]
    return total


def total_kernel(n_seq, n_fsdp, x_ref, out_ref, mid, slots_f, slots_s, sems_f, sems_s):
    meet(all_peers("seq", n_seq) + all_peers("fsdp", n_fsdp))
    mid[...] = exchange("fsdp", n_fsdp, x_ref, slots_f, sems_f)
    out_ref[...] = exchange("seq", n_seq, mid, slots_s, sems_s)


def total(n_seq, n_fsdp, x, collective_id):
    return pl.pallas_call(
        functools.partial(total_kernel, n_seq, n_fsdp),
        out_shape=jax.ShapeDtypeStruct(x.shape, x.dtype),
        in_specs=[pl.BlockSpec(memory_space=pltpu.VMEM)],
        out_specs=pl.BlockSpec(memory_space=pltpu.VMEM),
        scratch_shapes=[
            pltpu.VMEM(x.shape, x.dtype),
            pltpu.VMEM((n_fsdp,) + x.shape, x.dtype),
            pltpu.VMEM((n_seq,) + x.shape, x.dtype),
            pltpu.SemaphoreType.DMA((2, n_fsdp)),
            pltpu.SemaphoreType.DMA((2, n_seq)),
        ],
        compiler_params=pltpu.CompilerParams(
            collective_id=collective_id, has_side_effects=True, vmem_limit_bytes=VMEM_LIMIT
        ),
        name="total",
    )(x)


def body(
    n_seq, n_fsdp, tokens, norm_gain, router_weight, w_query, w_key, w_value, w_out, cotangent,
    kept_index
):
    own_rows, width = tokens.shape[1], tokens.shape[2]
    slot_list = kept_index[0, 0]
    cap = slot_list.shape[0]
    head_width = w_query.shape[1]
    slots = n_seq * cap
    is_kept = slot_list >= 0
    picked = jnp.where(is_kept, slot_list, 0)
    kept_rows = jnp.where(is_kept[:, None], tokens[0][picked], jnp.zeros((), jnp.bfloat16))
    kept_float = kept_rows.astype(jnp.float32)
    inv_root = lax.rsqrt(jnp.mean(kept_float * kept_float, axis=1) + EPS)
    unit = kept_float * inv_root[:, None]
    sending = (unit * norm_gain).astype(jnp.bfloat16)
    flags = jnp.zeros((128,), jnp.float32).at[:cap].set(is_kept.astype(jnp.float32))
    flags = jnp.broadcast_to(flags[None, :], (8, 128))
    seq, fsdp = ("seq", n_seq), ("fsdp", n_fsdp)
    rows_g, flags_g, query_g, key_g, value_g, out_g = gather(
        (seq, seq, fsdp, fsdp, fsdp, fsdp),
        (sending, flags, w_query, w_key, w_value, w_out),
        1,
    )
    all_rows = rows_g.reshape(slots, width)
    live = flags_g[:, 0, :cap].reshape(slots) > 0.5
    query_cols = query_g.reshape(width, head_width)
    key_cols = key_g.reshape(width, head_width)
    value_cols = value_g.reshape(width, head_width)
    out_full = jnp.swapaxes(out_g, 0, 1).reshape(head_width, width)
    queries = jnp.dot(all_rows, query_cols, preferred_element_type=jnp.float32).astype(jnp.bfloat16)
    keys_all = jnp.dot(all_rows, key_cols, preferred_element_type=jnp.float32).astype(jnp.bfloat16)
    values_all = jnp.dot(all_rows, value_cols, preferred_element_type=jnp.float32).astype(
        jnp.bfloat16
    )
    raw_scores = contract_cols(queries, keys_all) * QUERY_SCALE
    capped = SOFTCAP * jnp.tanh(raw_scores / SOFTCAP)
    order = jnp.arange(slots, dtype=jnp.int32)
    allowed = live[None, :] & ((order[None, :] <= order[:, None]) | ~live[:, None])
    powers = jnp.where(allowed, jnp.exp(capped), 0.0)
    softmax_values = powers / jnp.sum(powers, axis=1, keepdims=True)
    rounded_weights = softmax_values.astype(jnp.bfloat16)
    attended = jnp.dot(rounded_weights, values_all, preferred_element_type=jnp.float32).astype(
        jnp.bfloat16
    )
    (mixed_sum,) = reduce(
        (seq,),
        (1,),
        (
            jnp.dot(attended, out_full, preferred_element_type=jnp.float32)
            .astype(jnp.bfloat16)
            .reshape(n_seq, cap, width),
        ),
        2,
    )
    logits = jnp.dot(kept_float, router_weight, precision=lax.Precision.HIGHEST)
    gate_value = jax.nn.sigmoid(logits)
    cot_rows = jnp.where(
        is_kept[:, None], cotangent[0][picked], jnp.zeros((), jnp.bfloat16)
    ).astype(jnp.float32)
    d_mix = (gate_value[:, None] * cot_rows).astype(jnp.bfloat16)
    (d_mix_g,) = gather((seq,), (d_mix,), 3)
    d_mix_all = d_mix_g.reshape(slots, width)
    new_rows = (kept_float + gate_value[:, None] * mixed_sum).astype(jnp.bfloat16)
    target = jnp.where(is_kept, slot_list, own_rows)
    mixed_rows = tokens[0].at[target].set(new_rows, mode="drop")[None]
    d_gate = jnp.sum(cot_rows * mixed_sum, axis=1)
    d_logit = d_gate * gate_value * (1.0 - gate_value)
    out_part = contract_rows(attended, d_mix_all).astype(jnp.bfloat16)
    out_part = jnp.swapaxes(out_part.reshape(head_width, n_fsdp, width // n_fsdp), 0, 1)
    d_attended = contract_cols(d_mix_all, out_full).astype(jnp.bfloat16)
    d_values = contract_rows(rounded_weights, d_attended).astype(jnp.bfloat16)
    d_probs = contract_cols(d_attended, values_all)
    d_soft = softmax_values * (d_probs - jnp.sum(softmax_values * d_probs, axis=1, keepdims=True))
    d_raw = (d_soft * (1.0 - capped / SOFTCAP * (capped / SOFTCAP)) * QUERY_SCALE).astype(
        jnp.bfloat16
    )
    d_queries = jnp.dot(d_raw, keys_all, preferred_element_type=jnp.float32).astype(jnp.bfloat16)
    d_keys = contract_rows(d_raw, queries).astype(jnp.bfloat16)
    d_stack = jnp.concatenate([d_queries, d_keys, d_values], axis=1)
    stack_part = (
        contract_rows(all_rows, d_stack)
        .astype(jnp.bfloat16)
        .reshape(n_fsdp, width // n_fsdp, 3 * head_width)
    )
    total_in = contract_cols(d_queries, query_cols)
    total_in = total_in + contract_cols(d_keys, key_cols)
    normed_part = (
        (total_in + contract_cols(d_values, value_cols))
        .astype(jnp.bfloat16)
        .reshape(n_seq, cap, width)
    )
    d_normed, grad_query, grad_key, grad_value, out_grad = reduce(
        (seq, fsdp, fsdp), (1, 3, 1), (normed_part, stack_part, out_part), 4
    )
    gain_term = jnp.sum(d_normed * unit, axis=0)
    router_term = jnp.sum(d_logit[:, None] * kept_float, axis=0)
    sums = total(
        n_seq, n_fsdp, jnp.concatenate([gain_term, router_term]).reshape(2 * width // 128, 128), 5
    ).reshape(2 * width)
    grad_gain, grad_router = sums[:width], sums[width:]
    scaled = d_normed * norm_gain
    d_kept = inv_root[:, None] * (scaled - unit * jnp.mean(scaled * unit, axis=1, keepdims=True))
    grad_new = (cot_rows + d_kept + d_logit[:, None] * router_weight).astype(jnp.bfloat16)
    grad_tokens = cotangent[0].at[target].set(grad_new, mode="drop")[None]
    return (
        mixed_rows,
        grad_tokens,
        grad_query,
        grad_key,
        grad_value,
        out_grad,
        grad_gain,
        grad_router,
    )


def solution(mesh):
    in_specs = (
        P("fsdp", "seq", None),
        P(),
        P(),
        P("fsdp", "seq"),
        P("fsdp", "seq"),
        P("fsdp", "seq"),
        P("seq", "fsdp"),
        P("fsdp", "seq", None),
        P("fsdp", "seq", None),
    )
    out_specs = (
        P("fsdp", "seq", None),
        P("fsdp", "seq", None),
        P("fsdp", "seq"),
        P("fsdp", "seq"),
        P("fsdp", "seq"),
        P("seq", "fsdp"),
        P(),
        P(),
    )
    local = functools.partial(body, mesh.shape["seq"], mesh.shape["fsdp"])
    return jax.shard_map(
        local, mesh=mesh, in_specs=in_specs, out_specs=out_specs, check_vma=False
    )
```

```python
import functools

import jax
import jax.numpy as jnp
from jax import lax
from jax.experimental import pallas as pl
from jax.experimental.pallas import tpu as pltpu
from jax.sharding import PartitionSpec as P

SOFTCAP = 50.0
QUERY_SCALE = 1.0 / 12.0
EPS = 1e-06
MESH = pl.DeviceIdType.MESH
VMEM_LIMIT = 48 * 1024 * 1024


def contract_rows(left, right):
    return lax.dot_general(
        left, right, (((0,), (0,)), ((), ())), preferred_element_type=jnp.float32
    )


def contract_cols(left, right):
    return lax.dot_general(
        left, right, (((1,), (1,)), ((), ())), preferred_element_type=jnp.float32
    )


def place(axis, size):
    me = lax.axis_index(axis)
    return me, me // 2, lax.rem(me, 2), size // 2


def pair_peers(axis, size):
    me, outer, inner, outers = place(axis, size)
    peers = [{axis: lax.rem(outer + d, outers) * 2 + inner} for d in range(1, outers)]
    peers.append({axis: outer * 2 + 1 - inner})
    return peers


def all_peers(axis, size):
    me = lax.axis_index(axis)
    return [{axis: lax.rem(me + d, size)} for d in range(1, size)]


def meet(peers):
    barrier = pltpu.get_barrier_semaphore()
    for peer in peers:
        pl.semaphore_signal(barrier, inc=1, device_id=peer, device_id_type=MESH)
    pl.semaphore_wait(barrier, len(peers))


def remote(src, dst, send, recv, peer):
    return pltpu.make_async_remote_copy(
        src_ref=src, dst_ref=dst, send_sem=send, recv_sem=recv, device_id=peer, device_id_type=MESH
    )


def piece(ref, index, chunks, c):
    if chunks == 1:
        return ref.at[index]
    step = ref.shape[2] // chunks
    return ref.at[index, :, pl.ds(c * step, step)]


def gather_start(axis, size, src, dst, sems, chunks, c):
    me, outer, inner, outers = place(axis, size)
    step = src.shape[1] // chunks
    block = src if chunks == 1 else src.at[:, pl.ds(c * step, step)]
    land = piece(dst, me, chunks, c)
    first = []
    for d in range(1, outers):
        peer = {axis: lax.rem(outer + d, outers) * 2 + inner}
        first.append(remote(block, land, sems.at[0, d, c], sems.at[1, d, c], peer))
    partner = {axis: outer * 2 + 1 - inner}
    second = [remote(block, land, sems.at[2, 0, c], sems.at[3, 0, c], partner)]
    for copy in first + second:
        copy.start()
    return first, second


def gather_forward(axis, size, dst, sems, copies, chunks, c):
    me, outer, inner, outers = place(axis, size)
    first, second = copies
    partner = {axis: outer * 2 + 1 - inner}
    for d in range(1, outers):
        first[d - 1].wait_recv()
        land = piece(dst, lax.rem(outer + outers - d, outers) * 2 + inner, chunks, c)
        copy = remote(land, land, sems.at[2, d, c], sems.at[3, d, c], partner)
        copy.start()
        second.append(copy)


def gather_kernel(plan, order, *refs):
    count = len(plan)
    srcs, dsts = refs[:count], refs[count : 2 * count]
    sems, own_sems = refs[2 * count : 3 * count], refs[3 * count]
    peers = []
    for axis, size in dict(p[:2] for p in plan).items():
        peers += pair_peers(axis, size)
    meet(peers)
    running = []
    for i, c in order:
        axis, size, chunks = plan[i]
        running.append(gather_start(axis, size, srcs[i], dsts[i], sems[i], chunks, c))
    owns = []
    for i, (axis, size, _) in enumerate(plan):
        own = pltpu.make_async_copy(srcs[i], dsts[i].at[lax.axis_index(axis)], own_sems.at[i])
        own.start()
        owns.append(own)
    for (i, c), copies in zip(order, running):
        axis, size, chunks = plan[i]
        gather_forward(axis, size, dsts[i], sems[i], copies, chunks, c)
    for first, second in running:
        for copy in first:
            copy.wait_send()
        for copy in second:
            copy.wait()
    for own in owns:
        own.wait()


def gather(plan, order, arrays, collective_id):
    return pl.pallas_call(
        functools.partial(gather_kernel, plan, order),
        out_shape=[
            jax.ShapeDtypeStruct((p[1],) + a.shape, a.dtype) for p, a in zip(plan, arrays)
        ],
        in_specs=[pl.BlockSpec(memory_space=pl.ANY)] * len(arrays),
        out_specs=[pl.BlockSpec(memory_space=pl.ANY)] * len(arrays),
        scratch_shapes=[pltpu.SemaphoreType.DMA((4, size // 2, chunks)) for _, size, chunks in plan]
        + [pltpu.SemaphoreType.DMA((len(arrays),))],
        compiler_params=pltpu.CompilerParams(
            collective_id=collective_id, has_side_effects=True, vmem_limit_bytes=VMEM_LIMIT
        ),
        name="gather",
    )(*arrays)


def row_chunks(rows, run):
    if rows <= 32:
        run(slice(None))
        return
    step = next(s for s in (96, 64, 48, 32, 16) if rows % s == 0)

    @pl.loop(0, rows // step)
    def _(i):
        run(pl.ds(pl.multiple_of(i * step, step), step))


def scatter_start(axis, size, part, first_in, sems, d):
    me, outer, inner, outers = place(axis, size)
    to = lax.rem(outer + d, outers)
    copy = remote(
        part.at[to * 2 + 1 - inner],
        first_in.at[d],
        sems.at[0, d],
        sems.at[1, d],
        {axis: outer * 2 + 1 - inner},
    )
    copy.start()
    return copy


def scatter_step(axis, size, part, first_in, pair, second_in, sems, d, copy):
    me, outer, inner, outers = place(axis, size)
    to = lax.rem(outer + d, outers)
    copy.wait_recv()
    if d == 0:
        return None

    def run(rows):
        total = part[to * 2 + inner, rows].astype(jnp.float32) + first_in[d, rows].astype(
            jnp.float32
        )
        pair[d, rows] = total.astype(pair.dtype)

    row_chunks(part.shape[1], run)
    out = remote(
        pair.at[d], second_in.at[d], sems.at[2, d], sems.at[3, d], {axis: to * 2 + inner}
    )
    out.start()
    return out


def scatter_finish(axis, size, part, first_in, second_in, first, second, store):
    me, outer, inner, outers = place(axis, size)
    for copy in second:
        copy.wait()

    def run(rows):
        total = part[me, rows].astype(jnp.float32) + first_in[0, rows].astype(jnp.float32)
        for d in range(1, outers):
            total = total + second_in[d, rows].astype(jnp.float32)
        store(rows, total)

    row_chunks(part.shape[1], run)
    for _, copy in first:
        copy.wait_send()


def reduce_kernel(plan, splits, *refs):
    count, outs = len(plan), sum(splits)
    parts, out_refs, scratch = refs[:count], refs[count : count + outs], refs[count + outs :]
    peers = []
    for axis, size in dict(plan).items():
        peers += pair_peers(axis, size)
    meet(peers)
    held = [scratch[4 * i : 4 * i + 4] for i in range(count)]
    order = []
    for d in range(1, max(size for _, size in plan) // 2):
        order += [(i, d) for i, (_, size) in enumerate(plan) if d < size // 2]
    order += [(i, 0) for i in range(count)]
    firsts, seconds = [[] for _ in plan], [[] for _ in plan]
    sent = []
    for i, d in order:
        axis, size = plan[i]
        copy = scatter_start(axis, size, parts[i], held[i][0], held[i][3], d)
        firsts[i].append((d, copy))
        sent.append(copy)
    for (i, d), copy in zip(order, sent):
        axis, size = plan[i]
        first_in, pair, second_in, sems = held[i]
        out = scatter_step(axis, size, parts[i], first_in, pair, second_in, sems, d, copy)
        if out is not None:
            seconds[i].append(out)
    at = 0
    for i, (axis, size) in enumerate(plan):
        mine = out_refs[at : at + splits[i]]
        at += splits[i]

        def store(rows, total, mine=mine):
            width = total.shape[1] // len(mine)
            for j, ref in enumerate(mine):
                ref[rows] = total[:, j * width : (j + 1) * width]

        scatter_finish(
            axis, size, parts[i], held[i][0], held[i][2], firsts[i], seconds[i], store
        )


def reduce(plan, splits, arrays, collective_id):
    outs, scratch = [], []
    for (_, size), split, a in zip(plan, splits, arrays):
        outs += [jax.ShapeDtypeStruct((a.shape[1], a.shape[2] // split), jnp.float32)] * split
        scratch += [pltpu.VMEM((size // 2,) + a.shape[1:], a.dtype)] * 3
        scratch += [pltpu.SemaphoreType.DMA((4, size // 2))]
    return pl.pallas_call(
        functools.partial(reduce_kernel, plan, splits),
        out_shape=outs,
        in_specs=[pl.BlockSpec(memory_space=pltpu.VMEM)] * len(arrays),
        out_specs=[pl.BlockSpec(memory_space=pltpu.VMEM)] * len(outs),
        scratch_shapes=scratch,
        compiler_params=pltpu.CompilerParams(
            collective_id=collective_id, has_side_effects=True, vmem_limit_bytes=VMEM_LIMIT
        ),
        name="reduce",
    )(*arrays)


def exchange(axis, size, src, slots, sems):
    me = lax.axis_index(axis)
    copies = []
    for d in range(1, size):
        copies.append(
            remote(
                src, slots.at[me], sems.at[0, d], sems.at[1, d], {axis: lax.rem(me + d, size)}
            )
        )
    for copy in copies:
        copy.start()
    slots[me] = src[...]
    for copy in copies:
        copy.wait()
    total = slots[0]
    for s in range(1, size):
        total = total + slots[s]
    return total


def total_kernel(n_seq, n_fsdp, x_ref, out_ref, mid, slots_f, slots_s, sems_f, sems_s):
    meet(all_peers("seq", n_seq) + all_peers("fsdp", n_fsdp))
    mid[...] = exchange("fsdp", n_fsdp, x_ref, slots_f, sems_f)
    out_ref[...] = exchange("seq", n_seq, mid, slots_s, sems_s)


def total(n_seq, n_fsdp, x, collective_id):
    return pl.pallas_call(
        functools.partial(total_kernel, n_seq, n_fsdp),
        out_shape=jax.ShapeDtypeStruct(x.shape, x.dtype),
        in_specs=[pl.BlockSpec(memory_space=pltpu.VMEM)],
        out_specs=pl.BlockSpec(memory_space=pltpu.VMEM),
        scratch_shapes=[
            pltpu.VMEM(x.shape, x.dtype),
            pltpu.VMEM((n_fsdp,) + x.shape, x.dtype),
            pltpu.VMEM((n_seq,) + x.shape, x.dtype),
            pltpu.SemaphoreType.DMA((2, n_fsdp)),
            pltpu.SemaphoreType.DMA((2, n_seq)),
        ],
        compiler_params=pltpu.CompilerParams(
            collective_id=collective_id, has_side_effects=True, vmem_limit_bytes=VMEM_LIMIT
        ),
        name="total",
    )(x)


def body(
    n_seq, n_fsdp, tokens, norm_gain, router_weight, w_query, w_key, w_value, w_out, cotangent,
    kept_index
):
    own_rows, width = tokens.shape[1], tokens.shape[2]
    slot_list = kept_index[0, 0]
    cap = slot_list.shape[0]
    head_width = w_query.shape[1]
    slots = n_seq * cap
    is_kept = slot_list >= 0
    picked = jnp.where(is_kept, slot_list, 0)
    kept_rows = jnp.where(is_kept[:, None], tokens[0][picked], jnp.zeros((), jnp.bfloat16))
    kept_float = kept_rows.astype(jnp.float32)
    inv_root = lax.rsqrt(jnp.mean(kept_float * kept_float, axis=1) + EPS)
    unit = kept_float * inv_root[:, None]
    sending = (unit * norm_gain).astype(jnp.bfloat16)
    flags = jnp.zeros((128,), jnp.float32).at[:cap].set(is_kept.astype(jnp.float32))
    flags = jnp.broadcast_to(flags[None, :], (8, 128))
    logits = jnp.dot(kept_float, router_weight, precision=lax.Precision.HIGHEST)
    gate_value = jax.nn.sigmoid(logits)
    cot_rows = jnp.where(
        is_kept[:, None], cotangent[0][picked], jnp.zeros((), jnp.bfloat16)
    ).astype(jnp.float32)
    d_mix = (gate_value[:, None] * cot_rows).astype(jnp.bfloat16)
    seq, fsdp = ("seq", n_seq), ("fsdp", n_fsdp)
    rows_g, flags_g, query_g, key_g, value_g, out_g, d_mix_g = gather(
        (seq + (3,), seq + (1,), fsdp + (1,), fsdp + (1,), fsdp + (1,), fsdp + (1,), seq + (3,)),
        (
            (1, 0), (0, 0), (2, 0), (0, 1), (3, 0), (0, 2), (4, 0), (6, 0), (5, 0), (6, 1), (6, 2)
        ),
        (sending, flags, w_query, w_key, w_value, w_out, d_mix),
        1,
    )
    d_mix_all = d_mix_g.reshape(slots, width)
    all_rows = rows_g.reshape(slots, width)
    live = flags_g[:, 0, :cap].reshape(slots) > 0.5
    query_cols = query_g.reshape(width, head_width)
    key_cols = key_g.reshape(width, head_width)
    value_cols = value_g.reshape(width, head_width)
    out_full = jnp.swapaxes(out_g, 0, 1).reshape(head_width, width)
    queries = jnp.dot(all_rows, query_cols, preferred_element_type=jnp.float32).astype(jnp.bfloat16)
    keys_all = jnp.dot(all_rows, key_cols, preferred_element_type=jnp.float32).astype(jnp.bfloat16)
    values_all = jnp.dot(all_rows, value_cols, preferred_element_type=jnp.float32).astype(
        jnp.bfloat16
    )
    raw_scores = contract_cols(queries, keys_all) * QUERY_SCALE
    capped = SOFTCAP * jnp.tanh(raw_scores / SOFTCAP)
    order = jnp.arange(slots, dtype=jnp.int32)
    allowed = live[None, :] & ((order[None, :] <= order[:, None]) | ~live[:, None])
    powers = jnp.where(allowed, jnp.exp(capped), 0.0)
    softmax_values = powers / jnp.sum(powers, axis=1, keepdims=True)
    rounded_weights = softmax_values.astype(jnp.bfloat16)
    attended = jnp.dot(rounded_weights, values_all, preferred_element_type=jnp.float32).astype(
        jnp.bfloat16
    )
    mixed_part = (
        jnp.dot(attended, out_full, preferred_element_type=jnp.float32)
        .astype(jnp.bfloat16)
        .reshape(n_seq, cap, width)
    )
    out_part = contract_rows(attended, d_mix_all).astype(jnp.bfloat16)
    out_part = jnp.swapaxes(out_part.reshape(head_width, n_fsdp, width // n_fsdp), 0, 1)
    d_attended = contract_cols(d_mix_all, out_full).astype(jnp.bfloat16)
    d_values = contract_rows(rounded_weights, d_attended).astype(jnp.bfloat16)
    d_probs = contract_cols(d_attended, values_all)
    d_soft = softmax_values * (d_probs - jnp.sum(softmax_values * d_probs, axis=1, keepdims=True))
    d_raw = (d_soft * (1.0 - capped / SOFTCAP * (capped / SOFTCAP)) * QUERY_SCALE).astype(
        jnp.bfloat16
    )
    d_queries = jnp.dot(d_raw, keys_all, preferred_element_type=jnp.float32).astype(jnp.bfloat16)
    d_keys = contract_rows(d_raw, queries).astype(jnp.bfloat16)
    d_stack = jnp.concatenate([d_queries, d_keys, d_values], axis=1)
    stack_part = (
        contract_rows(all_rows, d_stack)
        .astype(jnp.bfloat16)
        .reshape(n_fsdp, width // n_fsdp, 3 * head_width)
    )
    total_in = contract_cols(d_queries, query_cols)
    total_in = total_in + contract_cols(d_keys, key_cols)
    normed_part = (
        (total_in + contract_cols(d_values, value_cols))
        .astype(jnp.bfloat16)
        .reshape(n_seq, cap, width)
    )
    mixed_sum, d_normed, grad_query, grad_key, grad_value, out_grad = reduce(
        (seq, seq, fsdp, fsdp),
        (1, 1, 3, 1),
        (mixed_part, normed_part, stack_part, out_part),
        2,
    )
    new_rows = (kept_float + gate_value[:, None] * mixed_sum).astype(jnp.bfloat16)
    target = jnp.where(is_kept, slot_list, own_rows)
    mixed_rows = tokens[0].at[target].set(new_rows, mode="drop")[None]
    d_gate = jnp.sum(cot_rows * mixed_sum, axis=1)
    d_logit = d_gate * gate_value * (1.0 - gate_value)
    gain_term = jnp.sum(d_normed * unit, axis=0)
    router_term = jnp.sum(d_logit[:, None] * kept_float, axis=0)
    sums = total(
        n_seq, n_fsdp, jnp.concatenate([gain_term, router_term]).reshape(2 * width // 128, 128), 3
    ).reshape(2 * width)
    grad_gain, grad_router = sums[:width], sums[width:]
    scaled = d_normed * norm_gain
    d_kept = inv_root[:, None] * (scaled - unit * jnp.mean(scaled * unit, axis=1, keepdims=True))
    grad_new = (cot_rows + d_kept + d_logit[:, None] * router_weight).astype(jnp.bfloat16)
    grad_tokens = cotangent[0].at[target].set(grad_new, mode="drop")[None]
    return (
        mixed_rows,
        grad_tokens,
        grad_query,
        grad_key,
        grad_value,
        out_grad,
        grad_gain,
        grad_router,
    )


def solution(mesh):
    in_specs = (
        P("fsdp", "seq", None),
        P(),
        P(),
        P("fsdp", "seq"),
        P("fsdp", "seq"),
        P("fsdp", "seq"),
        P("seq", "fsdp"),
        P("fsdp", "seq", None),
        P("fsdp", "seq", None),
    )
    out_specs = (
        P("fsdp", "seq", None),
        P("fsdp", "seq", None),
        P("fsdp", "seq"),
        P("fsdp", "seq"),
        P("fsdp", "seq"),
        P("seq", "fsdp"),
        P(),
        P(),
    )
    local = functools.partial(body, mesh.shape["seq"], mesh.shape["fsdp"])
    return jax.shard_map(
        local, mesh=mesh, in_specs=in_specs, out_specs=out_specs, check_vma=False
    )
```

```python
import functools

import jax
import jax.numpy as jnp
from jax import lax
from jax.experimental import pallas as pl
from jax.experimental.pallas import tpu as pltpu
from jax.sharding import PartitionSpec as P

SOFTCAP = 50.0
QUERY_SCALE = 1.0 / 12.0
EPS = 1e-06
MESH = pl.DeviceIdType.MESH
VMEM_LIMIT = 48 * 1024 * 1024


def contract_rows(left, right):
    return lax.dot_general(
        left, right, (((0,), (0,)), ((), ())), preferred_element_type=jnp.float32
    )


def contract_cols(left, right):
    return lax.dot_general(
        left, right, (((1,), (1,)), ((), ())), preferred_element_type=jnp.float32
    )


def place(axis, size):
    me = lax.axis_index(axis)
    return me, me // 2, lax.rem(me, 2), size // 2


def pair_peers(axis, size):
    me, outer, inner, outers = place(axis, size)
    peers = [{axis: lax.rem(outer + d, outers) * 2 + inner} for d in range(1, outers)]
    peers.append({axis: outer * 2 + 1 - inner})
    return peers


def all_peers(axis, size):
    me = lax.axis_index(axis)
    return [{axis: lax.rem(me + d, size)} for d in range(1, size)]


def meet(peers):
    barrier = pltpu.get_barrier_semaphore()
    for peer in peers:
        pl.semaphore_signal(barrier, inc=1, device_id=peer, device_id_type=MESH)
    pl.semaphore_wait(barrier, len(peers))


def remote(src, dst, send, recv, peer):
    return pltpu.make_async_remote_copy(
        src_ref=src, dst_ref=dst, send_sem=send, recv_sem=recv, device_id=peer, device_id_type=MESH
    )


def piece(ref, index, chunks, c):
    if chunks == 1:
        return ref.at[index]
    step = ref.shape[2] // chunks
    return ref.at[index, :, pl.ds(c * step, step)]


def gather_start(axis, size, src, dst, sems, chunks, c):
    me, outer, inner, outers = place(axis, size)
    step = src.shape[1] // chunks
    block = src if chunks == 1 else src.at[:, pl.ds(c * step, step)]
    land = piece(dst, me, chunks, c)
    first = []
    for d in range(1, outers):
        peer = {axis: lax.rem(outer + d, outers) * 2 + inner}
        first.append(remote(block, land, sems.at[0, d, c], sems.at[1, d, c], peer))
    partner = {axis: outer * 2 + 1 - inner}
    second = [remote(block, land, sems.at[2, 0, c], sems.at[3, 0, c], partner)]
    for copy in first + second:
        copy.start()
    return first, second


def gather_forward(axis, size, dst, sems, copies, chunks, c):
    me, outer, inner, outers = place(axis, size)
    first, second = copies
    partner = {axis: outer * 2 + 1 - inner}
    for d in range(1, outers):
        first[d - 1].wait_recv()
        land = piece(dst, lax.rem(outer + outers - d, outers) * 2 + inner, chunks, c)
        copy = remote(land, land, sems.at[2, d, c], sems.at[3, d, c], partner)
        copy.start()
        second.append(copy)


def gather_kernel(plan, order, *refs):
    count = len(plan)
    srcs, dsts = refs[:count], refs[count : 2 * count]
    sems, own_sems = refs[2 * count : 3 * count], refs[3 * count]
    peers = []
    for axis, size in dict(p[:2] for p in plan).items():
        peers += pair_peers(axis, size)
    meet(peers)
    running = []
    for i, c in order:
        axis, size, chunks = plan[i]
        running.append(gather_start(axis, size, srcs[i], dsts[i], sems[i], chunks, c))
    owns = []
    for i, (axis, size, _) in enumerate(plan):
        own = pltpu.make_async_copy(srcs[i], dsts[i].at[lax.axis_index(axis)], own_sems.at[i])
        own.start()
        owns.append(own)
    for (i, c), copies in zip(order, running):
        axis, size, chunks = plan[i]
        gather_forward(axis, size, dsts[i], sems[i], copies, chunks, c)
    for first, second in running:
        for copy in first:
            copy.wait_send()
        for copy in second:
            copy.wait()
    for own in owns:
        own.wait()


def gather(plan, order, arrays, collective_id):
    return pl.pallas_call(
        functools.partial(gather_kernel, plan, order),
        out_shape=[
            jax.ShapeDtypeStruct((p[1],) + a.shape, a.dtype) for p, a in zip(plan, arrays)
        ],
        in_specs=[pl.BlockSpec(memory_space=pl.ANY)] * len(arrays),
        out_specs=[pl.BlockSpec(memory_space=pl.ANY)] * len(arrays),
        scratch_shapes=[pltpu.SemaphoreType.DMA((4, size // 2, chunks)) for _, size, chunks in plan]
        + [pltpu.SemaphoreType.DMA((len(arrays),))],
        compiler_params=pltpu.CompilerParams(
            collective_id=collective_id, has_side_effects=True, vmem_limit_bytes=VMEM_LIMIT
        ),
        name="gather",
    )(*arrays)


def row_chunks(rows, run):
    if rows <= 32:
        run(slice(None))
        return
    step = next(s for s in (96, 64, 48, 32, 16) if rows % s == 0)

    @pl.loop(0, rows // step)
    def _(i):
        run(pl.ds(pl.multiple_of(i * step, step), step))


def scatter_start(axis, size, part, first_in, sems, d):
    me, outer, inner, outers = place(axis, size)
    to = lax.rem(outer + d, outers)
    copy = remote(
        part.at[to * 2 + 1 - inner],
        first_in.at[d],
        sems.at[0, d],
        sems.at[1, d],
        {axis: outer * 2 + 1 - inner},
    )
    copy.start()
    return copy


def scatter_step(axis, size, part, first_in, pair, second_in, sems, d, copy):
    me, outer, inner, outers = place(axis, size)
    to = lax.rem(outer + d, outers)
    copy.wait_recv()
    if d == 0:
        return None

    def run(rows):
        total = part[to * 2 + inner, rows].astype(jnp.float32) + first_in[d, rows].astype(
            jnp.float32
        )
        pair[d, rows] = total.astype(pair.dtype)

    row_chunks(part.shape[1], run)
    out = remote(
        pair.at[d], second_in.at[d], sems.at[2, d], sems.at[3, d], {axis: to * 2 + inner}
    )
    out.start()
    return out


def scatter_finish(axis, size, part, first_in, second_in, first, second, store):
    me, outer, inner, outers = place(axis, size)
    for copy in second:
        copy.wait()

    def run(rows):
        total = part[me, rows].astype(jnp.float32) + first_in[0, rows].astype(jnp.float32)
        for d in range(1, outers):
            total = total + second_in[d, rows].astype(jnp.float32)
        store(rows, total)

    row_chunks(part.shape[1], run)
    for _, copy in first:
        copy.wait_send()


def reduce_kernel(plan, splits, *refs):
    count, outs = len(plan), sum(splits)
    parts, out_refs, scratch = refs[:count], refs[count : count + outs], refs[count + outs :]
    peers = []
    for axis, size in dict(plan).items():
        peers += pair_peers(axis, size)
    meet(peers)
    held = [scratch[4 * i : 4 * i + 4] for i in range(count)]
    order = []
    for d in range(1, max(size for _, size in plan) // 2):
        order += [(i, d) for i, (_, size) in enumerate(plan) if d < size // 2]
    order += [(i, 0) for i in range(count)]
    firsts, seconds = [[] for _ in plan], [[] for _ in plan]
    sent = []
    for i, d in order:
        axis, size = plan[i]
        copy = scatter_start(axis, size, parts[i], held[i][0], held[i][3], d)
        firsts[i].append((d, copy))
        sent.append(copy)
    for (i, d), copy in zip(order, sent):
        axis, size = plan[i]
        first_in, pair, second_in, sems = held[i]
        out = scatter_step(axis, size, parts[i], first_in, pair, second_in, sems, d, copy)
        if out is not None:
            seconds[i].append(out)
    at = 0
    for i, (axis, size) in enumerate(plan):
        mine = out_refs[at : at + splits[i]]
        at += splits[i]

        def store(rows, total, mine=mine):
            width = total.shape[1] // len(mine)
            for j, ref in enumerate(mine):
                ref[rows] = total[:, j * width : (j + 1) * width]

        scatter_finish(
            axis, size, parts[i], held[i][0], held[i][2], firsts[i], seconds[i], store
        )


def reduce(plan, splits, arrays, collective_id):
    outs, scratch = [], []
    for (_, size), split, a in zip(plan, splits, arrays):
        outs += [jax.ShapeDtypeStruct((a.shape[1], a.shape[2] // split), jnp.float32)] * split
        scratch += [pltpu.VMEM((size // 2,) + a.shape[1:], a.dtype)] * 3
        scratch += [pltpu.SemaphoreType.DMA((4, size // 2))]
    return pl.pallas_call(
        functools.partial(reduce_kernel, plan, splits),
        out_shape=outs,
        in_specs=[pl.BlockSpec(memory_space=pltpu.VMEM)] * len(arrays),
        out_specs=[pl.BlockSpec(memory_space=pltpu.VMEM)] * len(outs),
        scratch_shapes=scratch,
        compiler_params=pltpu.CompilerParams(
            collective_id=collective_id, has_side_effects=True, vmem_limit_bytes=VMEM_LIMIT
        ),
        name="reduce",
    )(*arrays)


def exchange(axis, size, src, slots, sems):
    me = lax.axis_index(axis)
    copies = []
    for d in range(1, size):
        copies.append(
            remote(
                src, slots.at[me], sems.at[0, d], sems.at[1, d], {axis: lax.rem(me + d, size)}
            )
        )
    for copy in copies:
        copy.start()
    slots[me] = src[...]
    for copy in copies:
        copy.wait()
    total = slots[0]
    for s in range(1, size):
        total = total + slots[s]
    return total


def total_kernel(n_seq, n_fsdp, x_ref, out_ref, mid, slots_f, slots_s, sems_f, sems_s):
    meet(all_peers("seq", n_seq) + all_peers("fsdp", n_fsdp))
    mid[...] = exchange("fsdp", n_fsdp, x_ref, slots_f, sems_f)
    out_ref[...] = exchange("seq", n_seq, mid, slots_s, sems_s)


def total(n_seq, n_fsdp, x, collective_id):
    return pl.pallas_call(
        functools.partial(total_kernel, n_seq, n_fsdp),
        out_shape=jax.ShapeDtypeStruct(x.shape, x.dtype),
        in_specs=[pl.BlockSpec(memory_space=pltpu.VMEM)],
        out_specs=pl.BlockSpec(memory_space=pltpu.VMEM),
        scratch_shapes=[
            pltpu.VMEM(x.shape, x.dtype),
            pltpu.VMEM((n_fsdp,) + x.shape, x.dtype),
            pltpu.VMEM((n_seq,) + x.shape, x.dtype),
            pltpu.SemaphoreType.DMA((2, n_fsdp)),
            pltpu.SemaphoreType.DMA((2, n_seq)),
        ],
        compiler_params=pltpu.CompilerParams(
            collective_id=collective_id, has_side_effects=True, vmem_limit_bytes=VMEM_LIMIT
        ),
        name="total",
    )(x)


def middle_kernel(
    n_fsdp, rows, d_mix, allowed, w_query, w_key, w_value, w_out, mixed, normed, stack, out_grad,
    out_full
):
    head, width = out_full.shape
    share = width // n_fsdp
    low = jnp.bfloat16
    for f in range(n_fsdp):
        out_full[:, f * share : (f + 1) * share] = w_out[f]
    queries = jnp.dot(rows[...], w_query[...], preferred_element_type=jnp.float32).astype(low)
    keys = jnp.dot(rows[...], w_key[...], preferred_element_type=jnp.float32).astype(low)
    vals = jnp.dot(rows[...], w_value[...], preferred_element_type=jnp.float32).astype(low)
    slope = jnp.tanh(contract_cols(queries, keys) * (QUERY_SCALE / SOFTCAP))
    powers = jnp.where(allowed[...] > 0.5, jnp.exp(SOFTCAP * slope), 0.0)
    soft = powers / jnp.sum(powers, axis=1, keepdims=True)
    weights = soft.astype(low)
    attended = jnp.dot(weights, vals, preferred_element_type=jnp.float32).astype(low)
    d_attended = contract_cols(d_mix[...], out_full[...]).astype(low)
    d_values = contract_rows(weights, d_attended).astype(low)
    d_probs = contract_cols(d_attended, vals)
    d_soft = soft * (d_probs - jnp.sum(soft * d_probs, axis=1, keepdims=True))
    d_raw = (d_soft * (1.0 - slope * slope) * QUERY_SCALE).astype(low)
    d_queries = jnp.dot(d_raw, keys, preferred_element_type=jnp.float32).astype(low)
    d_keys = contract_rows(d_raw, queries).astype(low)
    d_stack = jnp.concatenate([d_queries, d_keys, d_values], axis=1)
    step = width // 6
    for c in range(6):
        part = slice(c * step, (c + 1) * step)
        mixed[:, part] = jnp.dot(
            attended, out_full[:, part], preferred_element_type=jnp.float32
        ).astype(low)
        in_cols = jnp.concatenate([w_query[part], w_key[part], w_value[part]], axis=1)
        normed[:, part] = contract_cols(d_stack, in_cols).astype(low)
        stack[part] = contract_rows(rows[:, part], d_stack).astype(low)
    grad = contract_rows(attended, d_mix[...]).astype(low)
    for f in range(n_fsdp):
        out_grad[f] = grad[:, f * share : (f + 1) * share]


def middle(n_fsdp, rows, d_mix, allowed, w_query, w_key, w_value, w_out):
    slots, width = rows.shape
    head = w_query.shape[1]
    low = jnp.bfloat16
    return pl.pallas_call(
        functools.partial(middle_kernel, n_fsdp),
        out_shape=[
            jax.ShapeDtypeStruct((slots, width), low),
            jax.ShapeDtypeStruct((slots, width), low),
            jax.ShapeDtypeStruct((width, 3 * head), low),
            jax.ShapeDtypeStruct((n_fsdp, head, width // n_fsdp), low),
        ],
        in_specs=[pl.BlockSpec(memory_space=pltpu.VMEM)] * 7,
        out_specs=[pl.BlockSpec(memory_space=pltpu.VMEM)] * 4,
        scratch_shapes=[pltpu.VMEM((head, width), low)],
        compiler_params=pltpu.CompilerParams(vmem_limit_bytes=VMEM_LIMIT),
        name="middle",
    )(rows, d_mix, allowed, w_query, w_key, w_value, w_out)


def body(
    n_seq, n_fsdp, tokens, norm_gain, router_weight, w_query, w_key, w_value, w_out, cotangent,
    kept_index
):
    own_rows, width = tokens.shape[1], tokens.shape[2]
    slot_list = kept_index[0, 0]
    cap = slot_list.shape[0]
    head_width = w_query.shape[1]
    slots = n_seq * cap
    is_kept = slot_list >= 0
    picked = jnp.where(is_kept, slot_list, 0)
    kept_rows = jnp.where(is_kept[:, None], tokens[0][picked], jnp.zeros((), jnp.bfloat16))
    kept_float = kept_rows.astype(jnp.float32)
    inv_root = lax.rsqrt(jnp.mean(kept_float * kept_float, axis=1) + EPS)
    unit = kept_float * inv_root[:, None]
    sending = (unit * norm_gain).astype(jnp.bfloat16)
    flags = jnp.zeros((128,), jnp.float32).at[:cap].set(is_kept.astype(jnp.float32))
    flags = jnp.broadcast_to(flags[None, :], (8, 128))
    logits = jnp.dot(kept_float, router_weight, precision=lax.Precision.HIGHEST)
    gate_value = jax.nn.sigmoid(logits)
    cot_rows = jnp.where(
        is_kept[:, None], cotangent[0][picked], jnp.zeros((), jnp.bfloat16)
    ).astype(jnp.float32)
    d_mix = (gate_value[:, None] * cot_rows).astype(jnp.bfloat16)
    seq, fsdp = ("seq", n_seq), ("fsdp", n_fsdp)
    rows_g, flags_g, query_g, key_g, value_g, out_g, d_mix_g = gather(
        (seq + (3,), seq + (1,), fsdp + (1,), fsdp + (1,), fsdp + (1,), fsdp + (1,), seq + (3,)),
        (
            (1, 0), (0, 0), (2, 0), (0, 1), (3, 0), (0, 2), (4, 0), (6, 0), (5, 0), (6, 1), (6, 2)
        ),
        (sending, flags, w_query, w_key, w_value, w_out, d_mix),
        1,
    )
    d_mix_all = d_mix_g.reshape(slots, width)
    all_rows = rows_g.reshape(slots, width)
    live = flags_g[:, 0, :cap].reshape(slots) > 0.5
    query_cols = query_g.reshape(width, head_width)
    key_cols = key_g.reshape(width, head_width)
    value_cols = value_g.reshape(width, head_width)
    order = jnp.arange(slots, dtype=jnp.int32)
    allowed = live[None, :] & ((order[None, :] <= order[:, None]) | ~live[:, None])
    mixed_part, normed_part, stack_part, out_part = middle(
        n_fsdp,
        all_rows,
        d_mix_all,
        allowed.astype(jnp.float32),
        query_cols,
        key_cols,
        value_cols,
        out_g,
    )
    mixed_part = mixed_part.reshape(n_seq, cap, width)
    normed_part = normed_part.reshape(n_seq, cap, width)
    stack_part = stack_part.reshape(n_fsdp, width // n_fsdp, 3 * head_width)
    mixed_sum, d_normed, grads, out_grad = reduce(
        (seq, seq, fsdp, fsdp),
        (1, 1, 1, 1),
        (mixed_part, normed_part, stack_part, out_part),
        2,
    )
    new_rows = (kept_float + gate_value[:, None] * mixed_sum).astype(jnp.bfloat16)
    target = jnp.where(is_kept, slot_list, own_rows)
    mixed_rows = tokens[0].at[target].set(new_rows, mode="drop")[None]
    d_gate = jnp.sum(cot_rows * mixed_sum, axis=1)
    d_logit = d_gate * gate_value * (1.0 - gate_value)
    gain_term = jnp.sum(d_normed * unit, axis=0)
    router_term = jnp.sum(d_logit[:, None] * kept_float, axis=0)
    sums = total(
        n_seq, n_fsdp, jnp.concatenate([gain_term, router_term]).reshape(2 * width // 128, 128), 3
    ).reshape(2 * width)
    grad_gain, grad_router = sums[:width], sums[width:]
    grad_query = grads[:, :head_width]
    grad_key = grads[:, head_width : 2 * head_width]
    grad_value = grads[:, 2 * head_width :]
    scaled = d_normed * norm_gain
    d_kept = inv_root[:, None] * (scaled - unit * jnp.mean(scaled * unit, axis=1, keepdims=True))
    grad_new = (cot_rows + d_kept + d_logit[:, None] * router_weight).astype(jnp.bfloat16)
    grad_tokens = cotangent[0].at[target].set(grad_new, mode="drop")[None]
    return (
        mixed_rows,
        grad_tokens,
        grad_query,
        grad_key,
        grad_value,
        out_grad,
        grad_gain,
        grad_router,
    )


def solution(mesh):
    in_specs = (
        P("fsdp", "seq", None),
        P(),
        P(),
        P("fsdp", "seq"),
        P("fsdp", "seq"),
        P("fsdp", "seq"),
        P("seq", "fsdp"),
        P("fsdp", "seq", None),
        P("fsdp", "seq", None),
    )
    out_specs = (
        P("fsdp", "seq", None),
        P("fsdp", "seq", None),
        P("fsdp", "seq"),
        P("fsdp", "seq"),
        P("fsdp", "seq"),
        P("seq", "fsdp"),
        P(),
        P(),
    )
    local = functools.partial(body, mesh.shape["seq"], mesh.shape["fsdp"])
    return jax.shard_map(
        local, mesh=mesh, in_specs=in_specs, out_specs=out_specs, check_vma=False
    )
```

```python
import functools

import jax
import jax.numpy as jnp
from jax import lax
from jax.experimental import pallas as pl
from jax.experimental.pallas import tpu as pltpu
from jax.sharding import PartitionSpec as P

SOFTCAP = 50.0
QUERY_SCALE = 1.0 / 12.0
EPS = 1e-06
MESH = pl.DeviceIdType.MESH
VMEM_LIMIT = 48 * 1024 * 1024


def contract_rows(left, right):
    return lax.dot_general(
        left, right, (((0,), (0,)), ((), ())), preferred_element_type=jnp.float32
    )


def contract_cols(left, right):
    return lax.dot_general(
        left, right, (((1,), (1,)), ((), ())), preferred_element_type=jnp.float32
    )


def place(axis, size):
    me = lax.axis_index(axis)
    return me, me // 2, lax.rem(me, 2), size // 2


def pair_peers(axis, size):
    me, outer, inner, outers = place(axis, size)
    peers = [{axis: lax.rem(outer + d, outers) * 2 + inner} for d in range(1, outers)]
    peers.append({axis: outer * 2 + 1 - inner})
    return peers


def all_peers(axis, size):
    me = lax.axis_index(axis)
    return [{axis: lax.rem(me + d, size)} for d in range(1, size)]


def meet(peers):
    barrier = pltpu.get_barrier_semaphore()
    for peer in peers:
        pl.semaphore_signal(barrier, inc=1, device_id=peer, device_id_type=MESH)
    pl.semaphore_wait(barrier, len(peers))


def remote(src, dst, send, recv, peer):
    return pltpu.make_async_remote_copy(
        src_ref=src, dst_ref=dst, send_sem=send, recv_sem=recv, device_id=peer, device_id_type=MESH
    )


def piece(ref, index, chunks, c):
    if chunks == 1:
        return ref.at[index]
    step = ref.shape[2] // chunks
    return ref.at[index, :, pl.ds(c * step, step)]


class Line:
    def __init__(self, axis, size, src, dst, sems, chunks, c, early):
        self.axis, self.dst, self.sems, self.chunks, self.c = axis, dst, sems, chunks, c
        self.me, self.outer, self.inner, self.outers = place(axis, size)
        step = src.shape[1] // chunks
        self.src = src if chunks == 1 else src.at[:, pl.ds(c * step, step)]
        self.kinds = (0, 1) if early else (0,)
        self.early = early
        self.partner = {axis: self.outer * 2 + 1 - self.inner}

    def land(self, kind, side, k):
        at = self.outer - k if side == 0 else self.outer + k
        parity = self.inner if kind == 0 else 1 - self.inner
        return piece(self.dst, at * 2 + parity, self.chunks, self.c)

    def have(self, side, k):
        return self.outer >= k if side == 0 else self.outer + k < self.outers

    def goes(self, side):
        return self.outer < self.outers - 1 if side == 0 else self.outer > 0

    def hop(self, kind, side, k):
        land = self.land(kind, side, k)
        to = self.outer + 1 if side == 0 else self.outer - 1
        return remote(
            self.src if kind == 0 and k == 0 else land,
            land,
            self.sems.at[kind, 2 * side, k, self.c],
            self.sems.at[kind, 2 * side + 1, k + 1, self.c],
            {self.axis: to * 2 + self.inner},
        )

    def arrival(self, kind, side, k):
        land = self.land(kind, side, k)
        return remote(
            land,
            land,
            self.sems.at[kind, 2 * side, k, self.c],
            self.sems.at[kind, 2 * side + 1, k, self.c],
            self.partner,
        )

    def across(self, side, k):
        land = self.land(0, side, k)
        return remote(
            self.src if k == 0 else land,
            land,
            self.sems.at[2, 2 * side, k, self.c],
            self.sems.at[2, 2 * side + 1, k, self.c],
            self.partner,
        )

    def across_arrival(self, side, k):
        land = self.land(1, side, k)
        return remote(
            land,
            land,
            self.sems.at[2, 2 * side, k, self.c],
            self.sems.at[2, 2 * side + 1, k, self.c],
            self.partner,
        )

    def start(self):
        self.across(0, 0).start()
        for side in (0, 1):
            pl.when(self.goes(side))(self.hop(0, side, 0).start)

    def step(self, k):
        if k == 0:
            if self.early:
                self.across_arrival(0, 0).wait_recv()
                for side in (0, 1):
                    pl.when(self.goes(side))(self.hop(1, side, 0).start)
            return
        for side in (0, 1):
            for kind in self.kinds:

                @pl.when(self.have(side, k))
                def _(side=side, kind=kind):
                    self.arrival(kind, side, k).wait_recv()
                    if k < self.outers - 1:
                        pl.when(self.goes(side))(self.hop(kind, side, k).start)
                    if not self.early:
                        self.across(side, k).start()

    def finish(self):
        self.across(0, 0).wait_send()
        if not self.early:
            self.across_arrival(0, 0).wait_recv()
        for side in (0, 1):
            for k in range(self.outers - 1):
                for kind in self.kinds:
                    pl.when(jnp.logical_and(self.have(side, k), self.goes(side)))(
                        self.hop(kind, side, k).wait_send
                    )
            if not self.early:
                for k in range(1, self.outers):

                    @pl.when(self.have(side, k))
                    def _(side=side, k=k):
                        self.across(side, k).wait_send()
                        self.across_arrival(side, k).wait_recv()


def meet_lines(sizes):
    barrier = pltpu.get_barrier_semaphore()
    count = 0
    for axis, size in sizes.items():
        me, outer, inner, outers = place(axis, size)
        pl.semaphore_signal(
            barrier, inc=1, device_id={axis: outer * 2 + 1 - inner}, device_id_type=MESH
        )
        for there, to in ((outer < outers - 1, outer + 1), (outer > 0, outer - 1)):

            @pl.when(there)
            def _(axis=axis, inner=inner, to=to):
                pl.semaphore_signal(
                    barrier, inc=1, device_id={axis: to * 2 + inner}, device_id_type=MESH
                )

            count = count + there.astype(jnp.int32)
        count = count + 1
    pl.semaphore_wait(barrier, count)


def gather_kernel(plan, order, *refs):
    count = len(plan)
    srcs, dsts = refs[:count], refs[count : 2 * count]
    sems, own_sems = refs[2 * count : 3 * count], refs[3 * count]
    meet_lines(dict(p[:2] for p in plan))
    lines = []
    for i, c in order:
        axis, size, chunks, early = plan[i]
        lines.append(Line(axis, size, srcs[i], dsts[i], sems[i], chunks, c, c < early))
    for line in lines:
        line.start()
    owns = []
    for i, p in enumerate(plan):
        own = pltpu.make_async_copy(srcs[i], dsts[i].at[lax.axis_index(p[0])], own_sems.at[i])
        own.start()
        owns.append(own)
    steps = [(j + k, j, k) for j, line in enumerate(lines) for k in range(line.outers)]
    for _, j, k in sorted(steps):
        lines[j].step(k)
    for line in lines:
        line.finish()
    for own in owns:
        own.wait()


def gather(plan, order, arrays, collective_id):
    return pl.pallas_call(
        functools.partial(gather_kernel, plan, order),
        out_shape=[
            jax.ShapeDtypeStruct((p[1],) + a.shape, a.dtype) for p, a in zip(plan, arrays)
        ],
        in_specs=[pl.BlockSpec(memory_space=pl.ANY)] * len(arrays),
        out_specs=[pl.BlockSpec(memory_space=pl.ANY)] * len(arrays),
        scratch_shapes=[
            pltpu.SemaphoreType.DMA((3, 4, p[1] // 2, p[2])) for p in plan
        ]
        + [pltpu.SemaphoreType.DMA((len(arrays),))],
        compiler_params=pltpu.CompilerParams(
            collective_id=collective_id, has_side_effects=True, vmem_limit_bytes=VMEM_LIMIT
        ),
        name="gather",
    )(*arrays)


def row_chunks(rows, run):
    if rows <= 32:
        run(slice(None))
        return
    step = next(s for s in (96, 64, 48, 32, 16) if rows % s == 0)

    @pl.loop(0, rows // step)
    def _(i):
        run(pl.ds(pl.multiple_of(i * step, step), step))


def scatter_start(axis, size, part, first_in, sems, d):
    me, outer, inner, outers = place(axis, size)
    to = lax.rem(outer + d, outers)
    copy = remote(
        part.at[to * 2 + 1 - inner],
        first_in.at[d],
        sems.at[0, d],
        sems.at[1, d],
        {axis: outer * 2 + 1 - inner},
    )
    copy.start()
    return copy


def scatter_step(axis, size, part, first_in, pair, second_in, sems, d, copy):
    me, outer, inner, outers = place(axis, size)
    to = lax.rem(outer + d, outers)
    copy.wait_recv()
    if d == 0:
        return None

    def run(rows):
        total = part[to * 2 + inner, rows].astype(jnp.float32) + first_in[d, rows].astype(
            jnp.float32
        )
        pair[d, rows] = total.astype(pair.dtype)

    row_chunks(part.shape[1], run)
    out = remote(
        pair.at[d], second_in.at[d], sems.at[2, d], sems.at[3, d], {axis: to * 2 + inner}
    )
    out.start()
    return out


def scatter_finish(axis, size, part, first_in, second_in, first, second, store):
    me, outer, inner, outers = place(axis, size)
    for copy in second:
        copy.wait()

    def run(rows):
        total = part[me, rows].astype(jnp.float32) + first_in[0, rows].astype(jnp.float32)
        for d in range(1, outers):
            total = total + second_in[d, rows].astype(jnp.float32)
        store(rows, total)

    row_chunks(part.shape[1], run)
    for _, copy in first:
        copy.wait_send()


def reduce_kernel(plan, splits, *refs):
    count, outs = len(plan), sum(splits)
    parts, out_refs, scratch = refs[:count], refs[count : count + outs], refs[count + outs :]
    peers = []
    for axis, size in dict(plan).items():
        peers += pair_peers(axis, size)
    meet(peers)
    held = [scratch[4 * i : 4 * i + 4] for i in range(count)]
    order = []
    for d in range(1, max(size for _, size in plan) // 2):
        order += [(i, d) for i, (_, size) in enumerate(plan) if d < size // 2]
    order += [(i, 0) for i in range(count)]
    firsts, seconds = [[] for _ in plan], [[] for _ in plan]
    sent = []
    for i, d in order:
        axis, size = plan[i]
        copy = scatter_start(axis, size, parts[i], held[i][0], held[i][3], d)
        firsts[i].append((d, copy))
        sent.append(copy)
    for (i, d), copy in zip(order, sent):
        axis, size = plan[i]
        first_in, pair, second_in, sems = held[i]
        out = scatter_step(axis, size, parts[i], first_in, pair, second_in, sems, d, copy)
        if out is not None:
            seconds[i].append(out)
    at = 0
    for i, (axis, size) in enumerate(plan):
        mine = out_refs[at : at + splits[i]]
        at += splits[i]

        def store(rows, total, mine=mine):
            width = total.shape[1] // len(mine)
            for j, ref in enumerate(mine):
                ref[rows] = total[:, j * width : (j + 1) * width]

        scatter_finish(
            axis, size, parts[i], held[i][0], held[i][2], firsts[i], seconds[i], store
        )


def reduce(plan, splits, arrays, collective_id):
    outs, scratch = [], []
    for (_, size), split, a in zip(plan, splits, arrays):
        outs += [jax.ShapeDtypeStruct((a.shape[1], a.shape[2] // split), jnp.float32)] * split
        scratch += [pltpu.VMEM((size // 2,) + a.shape[1:], a.dtype)] * 3
        scratch += [pltpu.SemaphoreType.DMA((4, size // 2))]
    return pl.pallas_call(
        functools.partial(reduce_kernel, plan, splits),
        out_shape=outs,
        in_specs=[pl.BlockSpec(memory_space=pltpu.VMEM)] * len(arrays),
        out_specs=[pl.BlockSpec(memory_space=pltpu.VMEM)] * len(outs),
        scratch_shapes=scratch,
        compiler_params=pltpu.CompilerParams(
            collective_id=collective_id, has_side_effects=True, vmem_limit_bytes=VMEM_LIMIT
        ),
        name="reduce",
    )(*arrays)


def exchange(axis, size, src, slots, sems):
    me = lax.axis_index(axis)
    copies = []
    for d in range(1, size):
        copies.append(
            remote(
                src, slots.at[me], sems.at[0, d], sems.at[1, d], {axis: lax.rem(me + d, size)}
            )
        )
    for copy in copies:
        copy.start()
    slots[me] = src[...]
    for copy in copies:
        copy.wait()
    total = slots[0]
    for s in range(1, size):
        total = total + slots[s]
    return total


def total_kernel(n_seq, n_fsdp, x_ref, out_ref, mid, slots_f, slots_s, sems_f, sems_s):
    meet(all_peers("seq", n_seq) + all_peers("fsdp", n_fsdp))
    mid[...] = exchange("fsdp", n_fsdp, x_ref, slots_f, sems_f)
    out_ref[...] = exchange("seq", n_seq, mid, slots_s, sems_s)


def total(n_seq, n_fsdp, x, collective_id):
    return pl.pallas_call(
        functools.partial(total_kernel, n_seq, n_fsdp),
        out_shape=jax.ShapeDtypeStruct(x.shape, x.dtype),
        in_specs=[pl.BlockSpec(memory_space=pltpu.VMEM)],
        out_specs=pl.BlockSpec(memory_space=pltpu.VMEM),
        scratch_shapes=[
            pltpu.VMEM(x.shape, x.dtype),
            pltpu.VMEM((n_fsdp,) + x.shape, x.dtype),
            pltpu.VMEM((n_seq,) + x.shape, x.dtype),
            pltpu.SemaphoreType.DMA((2, n_fsdp)),
            pltpu.SemaphoreType.DMA((2, n_seq)),
        ],
        compiler_params=pltpu.CompilerParams(
            collective_id=collective_id, has_side_effects=True, vmem_limit_bytes=VMEM_LIMIT
        ),
        name="total",
    )(x)


def middle_kernel(
    n_fsdp, rows, d_mix, allowed, w_query, w_key, w_value, w_out, mixed, normed, stack, out_grad,
    out_full
):
    head, width = out_full.shape
    share = width // n_fsdp
    low = jnp.bfloat16
    for f in range(n_fsdp):
        out_full[:, f * share : (f + 1) * share] = w_out[f]
    queries = jnp.dot(rows[...], w_query[...], preferred_element_type=jnp.float32).astype(low)
    keys = jnp.dot(rows[...], w_key[...], preferred_element_type=jnp.float32).astype(low)
    vals = jnp.dot(rows[...], w_value[...], preferred_element_type=jnp.float32).astype(low)
    slope = jnp.tanh(contract_cols(queries, keys) * (QUERY_SCALE / SOFTCAP))
    powers = jnp.where(allowed[...] > 0.5, jnp.exp(SOFTCAP * slope), 0.0)
    soft = powers / jnp.sum(powers, axis=1, keepdims=True)
    weights = soft.astype(low)
    attended = jnp.dot(weights, vals, preferred_element_type=jnp.float32).astype(low)
    d_attended = contract_cols(d_mix[...], out_full[...]).astype(low)
    d_values = contract_rows(weights, d_attended).astype(low)
    d_probs = contract_cols(d_attended, vals)
    d_soft = soft * (d_probs - jnp.sum(soft * d_probs, axis=1, keepdims=True))
    d_raw = (d_soft * (1.0 - slope * slope) * QUERY_SCALE).astype(low)
    d_queries = jnp.dot(d_raw, keys, preferred_element_type=jnp.float32).astype(low)
    d_keys = contract_rows(d_raw, queries).astype(low)
    d_stack = jnp.concatenate([d_queries, d_keys, d_values], axis=1)
    step = width // 6
    for c in range(6):
        part = slice(c * step, (c + 1) * step)
        mixed[:, part] = jnp.dot(
            attended, out_full[:, part], preferred_element_type=jnp.float32
        ).astype(low)
        in_cols = jnp.concatenate([w_query[part], w_key[part], w_value[part]], axis=1)
        normed[:, part] = contract_cols(d_stack, in_cols).astype(low)
        stack[part] = contract_rows(rows[:, part], d_stack).astype(low)
    grad = contract_rows(attended, d_mix[...]).astype(low)
    for f in range(n_fsdp):
        out_grad[f] = grad[:, f * share : (f + 1) * share]


def middle(n_fsdp, rows, d_mix, allowed, w_query, w_key, w_value, w_out):
    slots, width = rows.shape
    head = w_query.shape[1]
    low = jnp.bfloat16
    return pl.pallas_call(
        functools.partial(middle_kernel, n_fsdp),
        out_shape=[
            jax.ShapeDtypeStruct((slots, width), low),
            jax.ShapeDtypeStruct((slots, width), low),
            jax.ShapeDtypeStruct((width, 3 * head), low),
            jax.ShapeDtypeStruct((n_fsdp, head, width // n_fsdp), low),
        ],
        in_specs=[pl.BlockSpec(memory_space=pltpu.VMEM)] * 7,
        out_specs=[pl.BlockSpec(memory_space=pltpu.VMEM)] * 4,
        scratch_shapes=[pltpu.VMEM((head, width), low)],
        compiler_params=pltpu.CompilerParams(vmem_limit_bytes=VMEM_LIMIT),
        name="middle",
    )(rows, d_mix, allowed, w_query, w_key, w_value, w_out)


def body(
    n_seq, n_fsdp, tokens, norm_gain, router_weight, w_query, w_key, w_value, w_out, cotangent,
    kept_index
):
    own_rows, width = tokens.shape[1], tokens.shape[2]
    slot_list = kept_index[0, 0]
    cap = slot_list.shape[0]
    head_width = w_query.shape[1]
    slots = n_seq * cap
    is_kept = slot_list >= 0
    picked = jnp.where(is_kept, slot_list, 0)
    kept_rows = jnp.where(is_kept[:, None], tokens[0][picked], jnp.zeros((), jnp.bfloat16))
    kept_float = kept_rows.astype(jnp.float32)
    inv_root = lax.rsqrt(jnp.mean(kept_float * kept_float, axis=1) + EPS)
    unit = kept_float * inv_root[:, None]
    sending = (unit * norm_gain).astype(jnp.bfloat16)
    flags = jnp.zeros((128,), jnp.float32).at[:cap].set(is_kept.astype(jnp.float32))
    flags = jnp.broadcast_to(flags[None, :], (8, 128))
    logits = jnp.dot(kept_float, router_weight, precision=lax.Precision.HIGHEST)
    gate_value = jax.nn.sigmoid(logits)
    cot_rows = jnp.where(
        is_kept[:, None], cotangent[0][picked], jnp.zeros((), jnp.bfloat16)
    ).astype(jnp.float32)
    d_mix = (gate_value[:, None] * cot_rows).astype(jnp.bfloat16)
    seq, fsdp = ("seq", n_seq), ("fsdp", n_fsdp)
    rows_g, flags_g, query_g, key_g, value_g, out_g, d_mix_g = gather(
        (
            seq + (3, 1),
            seq + (1, 0),
            fsdp + (1, 0),
            fsdp + (1, 0),
            fsdp + (1, 0),
            fsdp + (1, 0),
            seq + (3, 1),
        ),
        (
            (0, 0), (1, 0), (2, 0), (0, 1), (3, 0), (0, 2), (4, 0), (6, 0), (5, 0), (6, 1), (6, 2)
        ),
        (sending, flags, w_query, w_key, w_value, w_out, d_mix),
        1,
    )
    d_mix_all = d_mix_g.reshape(slots, width)
    all_rows = rows_g.reshape(slots, width)
    live = flags_g[:, 0, :cap].reshape(slots) > 0.5
    query_cols = query_g.reshape(width, head_width)
    key_cols = key_g.reshape(width, head_width)
    value_cols = value_g.reshape(width, head_width)
    order = jnp.arange(slots, dtype=jnp.int32)
    allowed = live[None, :] & ((order[None, :] <= order[:, None]) | ~live[:, None])
    mixed_part, normed_part, stack_part, out_part = middle(
        n_fsdp,
        all_rows,
        d_mix_all,
        allowed.astype(jnp.float32),
        query_cols,
        key_cols,
        value_cols,
        out_g,
    )
    mixed_part = mixed_part.reshape(n_seq, cap, width)
    normed_part = normed_part.reshape(n_seq, cap, width)
    stack_part = stack_part.reshape(n_fsdp, width // n_fsdp, 3 * head_width)
    mixed_sum, d_normed, grads, out_grad = reduce(
        (seq, seq, fsdp, fsdp),
        (1, 1, 1, 1),
        (mixed_part, normed_part, stack_part, out_part),
        2,
    )
    new_rows = (kept_float + gate_value[:, None] * mixed_sum).astype(jnp.bfloat16)
    target = jnp.where(is_kept, slot_list, own_rows)
    mixed_rows = tokens[0].at[target].set(new_rows, mode="drop")[None]
    d_gate = jnp.sum(cot_rows * mixed_sum, axis=1)
    d_logit = d_gate * gate_value * (1.0 - gate_value)
    gain_term = jnp.sum(d_normed * unit, axis=0)
    router_term = jnp.sum(d_logit[:, None] * kept_float, axis=0)
    sums = total(
        n_seq, n_fsdp, jnp.concatenate([gain_term, router_term]).reshape(2 * width // 128, 128), 3
    ).reshape(2 * width)
    grad_gain, grad_router = sums[:width], sums[width:]
    grad_query = grads[:, :head_width]
    grad_key = grads[:, head_width : 2 * head_width]
    grad_value = grads[:, 2 * head_width :]
    scaled = d_normed * norm_gain
    d_kept = inv_root[:, None] * (scaled - unit * jnp.mean(scaled * unit, axis=1, keepdims=True))
    grad_new = (cot_rows + d_kept + d_logit[:, None] * router_weight).astype(jnp.bfloat16)
    grad_tokens = cotangent[0].at[target].set(grad_new, mode="drop")[None]
    return (
        mixed_rows,
        grad_tokens,
        grad_query,
        grad_key,
        grad_value,
        out_grad,
        grad_gain,
        grad_router,
    )


def solution(mesh):
    in_specs = (
        P("fsdp", "seq", None),
        P(),
        P(),
        P("fsdp", "seq"),
        P("fsdp", "seq"),
        P("fsdp", "seq"),
        P("seq", "fsdp"),
        P("fsdp", "seq", None),
        P("fsdp", "seq", None),
    )
    out_specs = (
        P("fsdp", "seq", None),
        P("fsdp", "seq", None),
        P("fsdp", "seq"),
        P("fsdp", "seq"),
        P("fsdp", "seq"),
        P("seq", "fsdp"),
        P(),
        P(),
    )
    local = functools.partial(body, mesh.shape["seq"], mesh.shape["fsdp"])
    return jax.shard_map(
        local, mesh=mesh, in_specs=in_specs, out_specs=out_specs, check_vma=False
    )
```
